32 devices in a mesh: chan: 4 (over x, core), tile: 8 (over z, y).
Axes of the slice: x: 2, y: 2, z: 4, core: 2. Of those that a mesh axis runs over, the one named last changes fastest.
Arguments:
- voltages: bfloat16 [4, 2, 2048, 2048], P(None, None, 'tile', 'chan'), may hold values from -16 to 16
- rfi_flags: int32 [4], P('chan'), may hold values 0 or 1
- beam_steer_index: int32 [4, 8], P('chan'), may hold values from 0 to 2047
- start_columns: int32 [4, 32], P('chan'), may hold values from 0 to 2047, as said below
Outputs:
- covariance: float32 [4, 2, 2048, 2048], P('chan', None, 'tile')
- weights: float32 [4, 8, 2, 2048], P('chan', None, None, 'tile')
The draws below stay inside these ranges and needn't reach their ends.
Inputs may be any that keep to these rules, and one draw needn't show every extreme that they name: `start_columns`: the 32 antenna numbers of one channel are distinct.
All inputs are finite; a program needn't handle non-finite values. No bound on the sum of `rfi_flags` on one device may be relied on, other than what follows from the above.
Results may differ from the reference program's by a relative error of at most 0.0003.
Values may be sent and summed in bfloat16 or wider, within the bound.
A program may use at most 128 MiB of HBM per device.

```python
import math
import jax
import jax.numpy as jnp
from jax import lax

ARRAY_ELEMENTS = 2048
SNAPSHOT_COUNT = 2048
SUBSPACE_SIZE = 32
SUB_ITERS = 4
CG_ITERS = 12
BEAM_COUNT = 8
CHANNEL_COUNT = 4


def draw_start_columns(key, part):
    channel_key_set = jax.random.split(jax.random.fold_in(key, 11), CHANNEL_COUNT)
    selected_beam = jax.vmap(lambda single_key: jax.random.permutation(single_key, ARRAY_ELEMENTS)[:SUBSPACE_SIZE])(channel_key_set)
    return selected_beam.astype(jnp.int32)


def draw_voltages(key, part):
    value_key = jax.random.fold_in(key, 23)
    jitter_key = jax.random.fold_in(key, 29)
    shape_full = (CHANNEL_COUNT, 2, SNAPSHOT_COUNT, ARRAY_ELEMENTS)
    position = jnp.arange(ARRAY_ELEMENTS, dtype=jnp.float32) / (ARRAY_ELEMENTS - 1)
    jitter = jnp.exp(jax.random.uniform(jitter_key, (ARRAY_ELEMENTS,), jnp.float32, jnp.log(0.8), jnp.log(1.25)))
    amplitude = jnp.exp(jnp.log(0.7) + (jnp.log(1.6) - jnp.log(0.7)) * position) * jitter
    values = jnp.clip(jax.random.normal(value_key, shape_full, jnp.float32), -6.0, 6.0)
    return (values * amplitude).astype(jnp.bfloat16)


def plant(drawn, own_key, smallest, largest):
    longest = drawn.shape.index(max(drawn.shape))
    spots = []
    for shift in (0, 1):
        where = [jax.random.randint(jax.random.fold_in(own_key, axis), (), 0, length) for axis, length in enumerate(drawn.shape)]
        where[longest] = (where[longest] + shift) % drawn.shape[longest]
        spots.append(tuple(where))
    return drawn.at[spots[0]].set(smallest).at[spots[1]].set(largest)


def setup_inputs(seed: int = 0) -> dict:
    arg_keys = jax.random.split(jax.random.key(seed), 5)
    return {
        "voltages": draw_voltages(jax.random.fold_in(arg_keys[4], 71), 0),
        "rfi_flags": plant((jax.random.randint(arg_keys[1], (CHANNEL_COUNT,), 0, 2) < 1).astype(jnp.int32), jax.random.fold_in(arg_keys[1], 1), 0, 1),
        "beam_steer_index": plant(jax.random.randint(arg_keys[2], (CHANNEL_COUNT, BEAM_COUNT), 0, ARRAY_ELEMENTS), jax.random.fold_in(arg_keys[2], 1), 0, ARRAY_ELEMENTS - 1).astype(jnp.int32),
        "start_columns": draw_start_columns(jax.random.fold_in(arg_keys[4], 71), 0),
    }


diagonal_loading = 0.1
highest = lax.Precision.HIGHEST

def steering_table(beam_entries):
    element_index = jnp.arange(ARRAY_ELEMENTS, dtype=jnp.int32)
    steer_phases = (beam_entries[..., None] * element_index % ARRAY_ELEMENTS).astype(jnp.float32) * (2.0 * math.pi / ARRAY_ELEMENTS)
    return jnp.stack([jnp.cos(steer_phases), jnp.sin(steer_phases)], axis=-2)

def orthonormal(vectors):
    dims_in = vectors.shape
    flattened = vectors.reshape(dims_in[:-2] + (dims_in[-2] * dims_in[-1],))
    gram_matrix = jnp.einsum('...kx,...lx->...kl', flattened, flattened, precision=highest)
    factor = jnp.linalg.cholesky(gram_matrix)
    solved = lax.linalg.triangular_solve(factor, flattened, left_side=True, lower=True)
    return solved.reshape(dims_in)

def apply_rows(covariance, vectors):
    upper_half = vectors[..., 0, :]
    lower_half = vectors[..., 1, :]
    stacked = jnp.stack([jnp.stack([upper_half, -lower_half], -2), jnp.stack([lower_half, upper_half], -2)], -3)
    return jnp.einsum('...bhpa,...pra->...bhr', stacked, covariance, precision=highest)

def project(vectors, subspace):
    coefficients = jnp.einsum('...bha,...kha->...bk', vectors, subspace, precision=highest)
    return vectors - jnp.einsum('...bk,...kha->...bha', coefficients, subspace, precision=highest)

def one_channel(arguments):
    voltage_block, flag_value, beam_entries, columns = arguments
    values = voltage_block.astype(jnp.float32)
    swapped = jnp.stack([values[1], -values[0]])
    real_part = jnp.einsum('psi,psj->ij', values, values, precision=highest)
    imag_part = jnp.einsum('psi,psj->ij', swapped, values, precision=highest)
    covariance = jnp.stack([real_part, imag_part]) * (1.0 / SNAPSHOT_COUNT)
    covariance_trace = jnp.sum(jnp.diagonal(covariance[0]))
    loading_amount = diagonal_loading * covariance_trace / ARRAY_ELEMENTS
    picked = covariance[:, :, columns]
    col_real = picked[0].T
    col_imag = picked[1].T
    first_block = jnp.concatenate([jnp.stack([col_real, col_imag], 1), jnp.stack([-col_imag, col_real], 1)], 0)
    subspace = orthonormal(first_block)
    for sweep_index in range(SUB_ITERS - 1):
        subspace = orthonormal(apply_rows(covariance, subspace))
    subspace = subspace * flag_value.astype(jnp.float32)
    steering = steering_table(beam_entries)

    def cg_sweep(counter, state_tuple):
        solved_weights, residual, direction, res_norm = state_tuple
        projected = project(direction, subspace)
        mapped = apply_rows(covariance, projected)
        combined = project(mapped, subspace) + loading_amount * direction
        curvature = jnp.sum(projected * mapped, axis=(1, 2)) + loading_amount * jnp.sum(direction * direction, axis=(1, 2))
        step_size = res_norm / curvature
        solved_weights = solved_weights + step_size[:, None, None] * direction
        residual = residual - step_size[:, None, None] * combined
        new_norm = jnp.sum(residual * residual, axis=(1, 2))
        direction = residual + (new_norm / res_norm)[:, None, None] * direction
        return (solved_weights, residual, direction, new_norm)
    start_state = (jnp.zeros_like(steering), steering, steering, jnp.sum(steering * steering, axis=(1, 2)))
    solved_weights = lax.fori_loop(0, CG_ITERS, cg_sweep, start_state)[0]
    array_response = jnp.sum(steering * solved_weights, axis=(1, 2))
    weights = ARRAY_ELEMENTS * solved_weights / array_response[:, None, None]
    return (covariance, weights)

def reference(voltages, rfi_flags, beam_steer_index, start_columns):
    covariance, weights = lax.map(one_channel, (voltages, rfi_flags, beam_steer_index, start_columns))
    return (covariance, weights)
```

```python
import functools
import math

import jax
import jax.numpy as jnp
from jax import lax
from jax.experimental import pallas as pl
from jax.experimental.pallas import tpu as pltpu
from jax.sharding import PartitionSpec as P

SUB_ITERS = 4
CG_ITERS = 12


diagonal_loading = 0.1
highest = lax.Precision.HIGHEST
MESH = pl.DeviceIdType.MESH


def steering_table(beam_entries, element_total):
    element_index = jnp.arange(element_total, dtype=jnp.int32)
    steer_phases = (beam_entries[..., None] * element_index % element_total).astype(
        jnp.float32
    ) * (2.0 * math.pi / element_total)
    return jnp.stack([jnp.cos(steer_phases), jnp.sin(steer_phases)], axis=0)


def dot_nt(a, b):
    return lax.dot_general(
        a, b, (((1,), (1,)), ((), ())), precision=highest, preferred_element_type=jnp.float32
    )


def dot_nn(a, b):
    return lax.dot_general(
        a, b, (((1,), (0,)), ((), ())), precision=highest, preferred_element_type=jnp.float32
    )


def dot_nt16(a, b):
    return lax.dot_general(a, b, (((1,), (1,)), ((), ())), preferred_element_type=jnp.float32)


def split_halves(values):
    high = values.astype(jnp.bfloat16)
    low = (values - high.astype(jnp.float32)).astype(jnp.bfloat16)
    return high, low


def complex_rows(product, count, rows):
    real = product[:count, :rows] - product[count:, rows:]
    imag = product[count:, :rows] + product[:count, rows:]
    return jnp.concatenate([real, imag], 0)


def embed(real, imag):
    return jnp.concatenate(
        [jnp.concatenate([real, -imag], 1), jnp.concatenate([imag, real], 1)], 0
    )


def hermitian_parts(product, count):
    real = product[:count, :count] + product[count:, count:]
    imag = product[count:, :count] - product[:count, count:]
    return real, imag


def inverse_factor(gram_real, gram_imag, count):
    row_id = lax.broadcasted_iota(jnp.int32, (count, count), 0)
    col_id = lax.broadcasted_iota(jnp.int32, (count, count), 1)
    eye = (row_id == col_id).astype(jnp.float32)
    system = jnp.concatenate([gram_real, gram_imag, eye, jnp.zeros_like(eye)], 1)
    below = lax.broadcasted_iota(jnp.int32, (count, 1), 0)
    lane = lax.broadcasted_iota(jnp.int32, (1, 4 * count), 1)
    first_half = lax.rem(lane, 2 * count) < count
    for k in range(count):
        row = system[k : k + 1, :]
        fore = pltpu.roll(row, 3 * count, 1)
        back = pltpu.roll(row, count, 1)
        turned = jnp.where(first_half, -fore, back)
        scale = jnp.where(below > k, 1.0 / row[:, k : k + 1], 0.0)
        factor_real = system[:, k : k + 1] * scale
        factor_imag = system[:, count + k : count + k + 1] * scale
        system = system - factor_real * row - factor_imag * turned
    pivots = jnp.sum(system[:, :count] * eye, axis=1, keepdims=True)
    system = system * lax.rsqrt(pivots)
    return embed(system[:, 2 * count : 3 * count], system[:, 3 * count :])


def tail_kernel(
    peers,
    cov_ref,
    columns_ref,
    flag_ref,
    steer_ref,
    out_ref,
    vectors,
    mapped,
    traces,
    factor_ref,
    basis_ref,
    wide_ref,
    high_ref,
    low_ref,
    x_ref,
    r_ref,
    p_ref,
    vec_send,
    vec_recv,
    map_send,
    map_recv,
    tr_send,
    tr_recv,
):
    me = lax.axis_index("tile")
    rows = cov_ref.shape[0] // 2
    antennas = cov_ref.shape[1]
    count = columns_ref.shape[1]
    beams = steer_ref.shape[0] // 2
    own = pl.ds(pl.multiple_of(me * rows, rows), rows)

    barrier = pltpu.get_barrier_semaphore()
    for k in range(1, peers):
        pl.semaphore_signal(
            barrier, inc=1, device_id={"tile": lax.rem(me + k, peers)}, device_id_type=MESH
        )
    pl.semaphore_wait(barrier, peers - 1)

    def send(block, send_sem, recv_sem):
        for k in range(1, peers):
            pltpu.make_async_remote_copy(
                src_ref=block.at[me],
                dst_ref=block.at[me],
                send_sem=send_sem.at[k],
                recv_sem=recv_sem.at[k],
                device_id={"tile": lax.rem(me + k, peers)},
                device_id_type=MESH,
            ).start()

    def arrive(block, send_sem, recv_sem):
        for k in range(1, peers):
            source = lax.rem(me - k + peers, peers)
            copy = pltpu.make_async_remote_copy(
                src_ref=block.at[me],
                dst_ref=block.at[source],
                send_sem=send_sem.at[k],
                recv_sem=recv_sem.at[k],
                device_id={"tile": lax.rem(me + k, peers)},
                device_id_type=MESH,
            )
            copy.wait_send()
            copy.wait_recv()

    def whole(block):
        return jnp.concatenate([block[j] for j in range(peers)], 1)

    hot = (
        lax.broadcasted_iota(jnp.int32, (antennas, count), 0) == columns_ref[0:1, :]
    ).astype(jnp.float32)
    picked = lax.dot_general(
        hot, cov_ref[...], (((0,), (1,)), ((), ())), precision=highest,
        preferred_element_type=jnp.float32,
    )
    vectors[0, me] = jnp.concatenate([picked[:, :rows], picked[:, rows:]], 0)
    send(vectors.at[0], vec_send.at[0], vec_recv.at[0])

    square = cov_ref[0:rows, own]
    on_diagonal = lax.broadcasted_iota(jnp.int32, (rows, rows), 0) == lax.broadcasted_iota(
        jnp.int32, (rows, rows), 1
    )
    own_trace = jnp.sum(jnp.where(on_diagonal, square, 0.0), axis=(0, 1), keepdims=True)
    traces[me] = jnp.broadcast_to(own_trace, traces.shape[1:])
    send(traces, tr_send, tr_recv)

    def subspace_round(step, carry):
        now, later = lax.rem(step, 2), lax.rem(step + 1, 2)
        arrive(vectors.at[now], vec_send.at[now], vec_recv.at[now])
        block = whole(vectors.at[now])
        moved = complex_rows(dot_nt(block, cov_ref[...]), count, rows)
        factor = inverse_factor(*hermitian_parts(dot_nt(block, block), count), count)
        factor_ref[...] = factor
        vectors[later, me] = dot_nn(factor, moved)
        send(vectors.at[later], vec_send.at[later], vec_recv.at[later])
        return carry

    lax.fori_loop(0, SUB_ITERS, subspace_round, 0)
    last, after = (SUB_ITERS - 1) % 2, SUB_ITERS % 2
    flag = flag_ref[...].astype(jnp.float32)
    basis = dot_nn(factor_ref[...], whole(vectors.at[last])) * flag
    basis_ref[...] = basis
    arrive(vectors.at[after], vec_send.at[after], vec_recv.at[after])
    image = whole(vectors.at[after]) * flag
    inner = embed(*hermitian_parts(dot_nt(image, basis), count))
    wide_ref[0 : 2 * count, :] = image - 0.5 * dot_nn(inner, basis)
    wide_ref[2 * count :, :] = basis
    own_basis = basis_ref[:, own]
    own_wide = wide_ref[0 : 2 * count, own]
    left_real = jnp.concatenate([own_basis, own_wide], 0)
    left_imag = jnp.concatenate(
        [own_basis[count:], -own_basis[:count], own_wide[count:], -own_wide[:count]], 0
    )
    left = jnp.concatenate([left_real.T, left_imag.T], 0)

    @pl.loop(0, peers)
    def _(j):
        part = pl.ds(pl.multiple_of(j * rows, rows), rows)
        projected = cov_ref[:, part] - dot_nn(left, wide_ref[:, part])
        high, low = split_halves(projected)
        high_ref[:, part] = high
        low_ref[:, part] = low

    arrive(traces, tr_send, tr_recv)
    trace = traces[0, 0:1, 0:1]
    for j in range(1, peers):
        trace = trace + traces[j, 0:1, 0:1]
    load = diagonal_loading * trace / antennas

    def inner_product(a, b):
        each = jnp.sum(a * b, axis=1, keepdims=True)
        return each[:beams] + each[beams:]

    def both(each):
        return jnp.concatenate([each, each], 0)

    steering = steer_ref[...]
    x_ref[...] = jnp.zeros_like(steering)
    r_ref[...] = steering
    p_ref[...] = steering

    def cg_step(step, norm):
        slot = lax.rem(step, 2)
        direction = p_ref[...]
        high, low = split_halves(direction)
        top = dot_nt16(jnp.concatenate([high, low], 0), high_ref[...])
        product = top[: 2 * beams] + top[2 * beams :] + dot_nt16(high, low_ref[...])
        mapped[slot, me] = complex_rows(product, beams, rows)
        send(mapped.at[slot], map_send.at[slot], map_recv.at[slot])
        arrive(mapped.at[slot], map_send.at[slot], map_recv.at[slot])
        combined = whole(mapped.at[slot]) + load * direction
        alpha = norm / inner_product(direction, combined)
        alpha_rows = both(alpha)
        x_ref[...] = x_ref[...] + alpha_rows * direction
        residual = r_ref[...] - alpha_rows * combined
        r_ref[...] = residual
        new_norm = inner_product(residual, residual)
        p_ref[...] = residual + both(new_norm / norm) * direction
        return new_norm

    lax.fori_loop(0, CG_ITERS, cg_step, inner_product(steering, steering))
    response = both(inner_product(steer_ref[...], x_ref[...]))
    out_ref[...] = antennas * x_ref[:, own] / response


def beam_weights(covariance, rfi_flags, beam_steer_index, start_columns):
    peers = lax.axis_size("tile")
    _, _, rows, antennas = covariance.shape
    beams = beam_steer_index.shape[1]
    count = start_columns.shape[1]
    steering = steering_table(beam_steer_index[0], antennas).reshape(2 * beams, antennas)
    f32, b16 = jnp.float32, jnp.bfloat16
    dma = pltpu.SemaphoreType.DMA
    out = pl.pallas_call(
        functools.partial(tail_kernel, peers),
        out_shape=jax.ShapeDtypeStruct((2 * beams, rows), f32),
        in_specs=[pl.BlockSpec(memory_space=pltpu.VMEM)] * 4,
        out_specs=pl.BlockSpec(memory_space=pltpu.VMEM),
        scratch_shapes=[
            pltpu.VMEM((2, peers, 2 * count, rows), f32),
            pltpu.VMEM((2, peers, 2 * beams, rows), f32),
            pltpu.VMEM((peers, 8, 128), f32),
            pltpu.VMEM((2 * count, 2 * count), f32),
            pltpu.VMEM((2 * count, antennas), f32),
            pltpu.VMEM((4 * count, antennas), f32),
            pltpu.VMEM((2 * rows, antennas), b16),
            pltpu.VMEM((2 * rows, antennas), b16),
            pltpu.VMEM((2 * beams, antennas), f32),
            pltpu.VMEM((2 * beams, antennas), f32),
            pltpu.VMEM((2 * beams, antennas), f32),
            dma((2, peers)),
            dma((2, peers)),
            dma((2, peers)),
            dma((2, peers)),
            dma((peers,)),
            dma((peers,)),
        ],
        compiler_params=pltpu.CompilerParams(
            collective_id=0, has_side_effects=True, vmem_limit_bytes=48 * 1024 * 1024
        ),
    )(
        covariance.reshape(2 * rows, antennas),
        start_columns,
        rfi_flags.reshape(1, 1),
        steering,
    )
    return jnp.swapaxes(out.reshape(2, beams, rows), 0, 1)[None]


def shards(voltages, rfi_flags, beam_steer_index, start_columns):
    turned = lax.all_to_all(voltages, "chan", split_axis=0, concat_axis=3, tiled=True)
    snapshots = voltages.shape[2] * lax.axis_size("tile")
    rows = turned.shape[3] // lax.axis_size("tile")
    first_row = lax.axis_index("tile") * rows
    gathered = lax.all_gather(turned, "tile", axis=2, tiled=True)
    own_rows = lax.dynamic_slice_in_dim(gathered, first_row, rows, 3)
    swapped = jnp.stack([own_rows[:, 1], -own_rows[:, 0]], 1)
    real_part = jnp.einsum("cpsi,cpsj->cij", own_rows, gathered, preferred_element_type=jnp.float32)
    imag_part = jnp.einsum("cpsi,cpsj->cij", swapped, gathered, preferred_element_type=jnp.float32)
    covariance = jnp.stack([real_part, imag_part], 1) * (1.0 / snapshots)
    weights = beam_weights(covariance, rfi_flags, beam_steer_index, start_columns)
    return (covariance, weights)


def solution(mesh):
    in_specs = (P(None, None, "tile", "chan"), P("chan"), P("chan", None), P("chan", None))
    out_specs = (P("chan", None, "tile", None), P("chan", None, None, "tile"))
    return jax.shard_map(shards, mesh=mesh, in_specs=in_specs, out_specs=out_specs, check_vma=False)
```

```python
import functools
import math

import jax
import jax.numpy as jnp
from jax import lax
from jax.experimental import pallas as pl
from jax.experimental.pallas import tpu as pltpu
from jax.sharding import PartitionSpec as P

SUB_ITERS = 4
CG_ITERS = 12


diagonal_loading = 0.1
highest = lax.Precision.HIGHEST
MESH = pl.DeviceIdType.MESH


def steering_table(beam_entries, element_total):
    element_index = jnp.arange(element_total, dtype=jnp.int32)
    steer_phases = (beam_entries[..., None] * element_index % element_total).astype(
        jnp.float32
    ) * (2.0 * math.pi / element_total)
    return jnp.stack([jnp.cos(steer_phases), jnp.sin(steer_phases)], axis=0)


def dot_nt(a, b):
    return lax.dot_general(
        a, b, (((1,), (1,)), ((), ())), precision=highest, preferred_element_type=jnp.float32
    )


def dot_nn(a, b):
    return lax.dot_general(
        a, b, (((1,), (0,)), ((), ())), precision=highest, preferred_element_type=jnp.float32
    )


def dot_nt16(a, b):
    return lax.dot_general(a, b, (((1,), (1,)), ((), ())), preferred_element_type=jnp.float32)


def split_halves(values):
    high = values.astype(jnp.bfloat16)
    low = (values - high.astype(jnp.float32)).astype(jnp.bfloat16)
    return high, low


def complex_rows(product, count, rows):
    real = product[:count, :rows] - product[count:, rows:]
    imag = product[count:, :rows] + product[:count, rows:]
    return jnp.concatenate([real, imag], 0)


def embed(real, imag):
    return jnp.concatenate(
        [jnp.concatenate([real, -imag], 1), jnp.concatenate([imag, real], 1)], 0
    )


def hermitian_parts(product, count):
    real = product[:count, :count] + product[count:, count:]
    imag = product[count:, :count] - product[:count, count:]
    return real, imag


def inverse_factor(gram_real, gram_imag, count):
    row_id = lax.broadcasted_iota(jnp.int32, (count, count), 0)
    col_id = lax.broadcasted_iota(jnp.int32, (count, count), 1)
    eye = (row_id == col_id).astype(jnp.float32)
    system = jnp.concatenate([gram_real, gram_imag, eye, jnp.zeros_like(eye)], 1)
    below = lax.broadcasted_iota(jnp.int32, (count, 1), 0)
    lane = lax.broadcasted_iota(jnp.int32, (1, 4 * count), 1)
    first_half = lax.rem(lane, 2 * count) < count
    for k in range(count):
        row = system[k : k + 1, :]
        fore = pltpu.roll(row, 3 * count, 1)
        back = pltpu.roll(row, count, 1)
        turned = jnp.where(first_half, -fore, back)
        scale = jnp.where(below > k, 1.0 / row[:, k : k + 1], 0.0)
        factor_real = system[:, k : k + 1] * scale
        factor_imag = system[:, count + k : count + k + 1] * scale
        system = system - factor_real * row - factor_imag * turned
    pivots = jnp.sum(system[:, :count] * eye, axis=1, keepdims=True)
    system = system * lax.rsqrt(pivots)
    return embed(system[:, 2 * count : 3 * count], system[:, 3 * count :])


def ring_place(position, peers):
    half = peers // 2
    return jnp.where(position < half, 2 * position, 2 * (peers - 1 - position) + 1)


def covariance_kernel(
    peers, groups, volt_ref, cov_ref, shards_ref, left_ref, local_sem, turn_send, turn_recv, ring_send, ring_recv
):
    me = lax.axis_index("tile")
    chan = lax.axis_index("chan")
    _, _, depth, width = volt_ref.shape
    rows = cov_ref.shape[0] // 2
    antennas = cov_ref.shape[1]
    half = peers // 2
    own = pl.ds(pl.multiple_of(me * rows, rows), rows)
    odd = lax.rem(me, 2)
    position = jnp.where(odd == 0, me // 2, peers - 1 - me // 2)

    def tile_at(offset):
        return ring_place(lax.rem(position + offset + peers, peers), peers)

    right, left = tile_at(1), tile_at(-1)

    barrier = pltpu.get_barrier_semaphore()
    for k in range(1, groups):
        pl.semaphore_signal(
            barrier, inc=1, device_id={"chan": lax.rem(chan + k, groups)}, device_id_type=MESH
        )
    for neighbour in (left, right):
        pl.semaphore_signal(barrier, inc=1, device_id={"tile": neighbour}, device_id_type=MESH)
    pl.semaphore_wait(barrier, groups + 1)

    def piece(tile, source):
        lanes = pl.ds(pl.multiple_of(source * width, width), width)
        return shards_ref.at[tile, :, :, lanes]

    def turn_copy(k):
        return pltpu.make_async_remote_copy(
            src_ref=volt_ref.at[lax.rem(chan + k, groups)],
            dst_ref=piece(me, chan),
            send_sem=turn_send.at[k],
            recv_sem=turn_recv.at[k],
            device_id={"chan": lax.rem(chan + k, groups)},
            device_id_type=MESH,
        )

    def turn_arrival(k):
        source = lax.rem(chan - k + groups, groups)
        return pltpu.make_async_remote_copy(
            src_ref=volt_ref.at[chan],
            dst_ref=piece(me, source),
            send_sem=turn_send.at[k],
            recv_sem=turn_recv.at[k],
            device_id={"chan": lax.rem(chan + k, groups)},
            device_id_type=MESH,
        )

    def hops(way, k):
        longer = 0 if k < groups // 2 else 1
        return half if way == longer else half - 1

    def ring_copy(way, hop, k, arriving=False):
        step = 1 if way == 0 else -1
        tile = tile_at(-step * (hop + 1 if arriving else hop))
        part = piece(tile, lax.rem(chan - k + groups, groups))
        return pltpu.make_async_remote_copy(
            src_ref=part,
            dst_ref=part,
            send_sem=ring_send.at[way, hop, k],
            recv_sem=ring_recv.at[way, hop, k],
            device_id={"tile": right if way == 0 else left},
            device_id_type=MESH,
        )

    def add_shard(tile, first=False, scale=None):
        real, imag = shards_ref[tile, 0, :, own], shards_ref[tile, 1, :, own]
        left_ref[...] = jnp.concatenate(
            [jnp.concatenate([real, imag], 1), jnp.concatenate([imag, -real], 1)], 0
        ).T

        @pl.loop(0, peers)
        def _(j):
            part = pl.ds(pl.multiple_of(j * rows, rows), rows)
            right_part = jnp.concatenate(
                [shards_ref[tile, 0, :, part], shards_ref[tile, 1, :, part]], 0
            )
            term = jnp.dot(left_ref[...], right_part, preferred_element_type=jnp.float32)
            if not first:
                term = term + cov_ref[:, part]
            if scale is not None:
                term = term * scale
            cov_ref[:, part] = term

    local = pltpu.make_async_copy(volt_ref.at[chan], piece(me, chan), local_sem)
    for k in range(1, groups):
        turn_copy(k).start()
    local.start()
    for k in range(groups):
        if k == 0:
            local.wait()
        else:
            turn_arrival(k).wait_recv()
        for way in range(2):
            ring_copy(way, 0, k).start()
    add_shard(me, first=True)
    for hop in range(half):
        for k in range(groups):
            for way in range(2):
                if hop < hops(way, k):
                    ring_copy(way, hop, k, arriving=True).wait_recv()
                    if hop + 1 < hops(way, k):
                        ring_copy(way, hop + 1, k).start()
        if hop + 1 < half:
            add_shard(tile_at(-hop - 1))
            add_shard(tile_at(hop + 1))
        else:
            add_shard(tile_at(half), scale=1.0 / (depth * peers))
    for k in range(1, groups):
        turn_copy(k).wait_send()
    for k in range(groups):
        for way in range(2):
            for hop in range(hops(way, k)):
                ring_copy(way, hop, k).wait_send()


def channel_covariance(voltages):
    peers, groups = lax.axis_size("tile"), lax.axis_size("chan")
    _, _, depth, width = voltages.shape
    antennas = width * groups
    rows = antennas // peers
    dma = pltpu.SemaphoreType.DMA
    out = pl.pallas_call(
        functools.partial(covariance_kernel, peers, groups),
        out_shape=jax.ShapeDtypeStruct((2 * rows, antennas), jnp.float32),
        in_specs=[pl.BlockSpec(memory_space=pl.ANY)],
        out_specs=pl.BlockSpec(memory_space=pltpu.VMEM),
        scratch_shapes=[
            pltpu.VMEM((peers, 2, depth, antennas), voltages.dtype),
            pltpu.VMEM((2 * rows, 2 * depth), voltages.dtype),
            dma(()),
            dma((groups,)),
            dma((groups,)),
            dma((2, peers // 2, groups)),
            dma((2, peers // 2, groups)),
        ],
        compiler_params=pltpu.CompilerParams(
            collective_id=1, has_side_effects=True, vmem_limit_bytes=40 * 1024 * 1024
        ),
    )(voltages)
    return out.reshape(1, 2, rows, antennas)


def tail_kernel(
    peers,
    cov_ref,
    columns_ref,
    flag_ref,
    steer_ref,
    out_ref,
    vectors,
    mapped,
    traces,
    factor_ref,
    basis_ref,
    wide_ref,
    high_ref,
    low_ref,
    x_ref,
    r_ref,
    p_ref,
    vec_send,
    vec_recv,
    map_send,
    map_recv,
    tr_send,
    tr_recv,
):
    me = lax.axis_index("tile")
    rows = cov_ref.shape[0] // 2
    antennas = cov_ref.shape[1]
    count = columns_ref.shape[1]
    beams = steer_ref.shape[0] // 2
    own = pl.ds(pl.multiple_of(me * rows, rows), rows)

    barrier = pltpu.get_barrier_semaphore()
    for k in range(1, peers):
        pl.semaphore_signal(
            barrier, inc=1, device_id={"tile": lax.rem(me + k, peers)}, device_id_type=MESH
        )
    pl.semaphore_wait(barrier, peers - 1)

    def send(block, send_sem, recv_sem):
        for k in range(1, peers):
            pltpu.make_async_remote_copy(
                src_ref=block.at[me],
                dst_ref=block.at[me],
                send_sem=send_sem.at[k],
                recv_sem=recv_sem.at[k],
                device_id={"tile": lax.rem(me + k, peers)},
                device_id_type=MESH,
            ).start()

    def arrive(block, send_sem, recv_sem):
        for k in range(1, peers):
            source = lax.rem(me - k + peers, peers)
            copy = pltpu.make_async_remote_copy(
                src_ref=block.at[me],
                dst_ref=block.at[source],
                send_sem=send_sem.at[k],
                recv_sem=recv_sem.at[k],
                device_id={"tile": lax.rem(me + k, peers)},
                device_id_type=MESH,
            )
            copy.wait_send()
            copy.wait_recv()

    def whole(block):
        return jnp.concatenate([block[j] for j in range(peers)], 1)

    hot = (
        lax.broadcasted_iota(jnp.int32, (antennas, count), 0) == columns_ref[0:1, :]
    ).astype(jnp.float32)
    picked = lax.dot_general(
        hot, cov_ref[...], (((0,), (1,)), ((), ())), precision=highest,
        preferred_element_type=jnp.float32,
    )
    vectors[0, me] = jnp.concatenate([picked[:, :rows], picked[:, rows:]], 0)
    send(vectors.at[0], vec_send.at[0], vec_recv.at[0])

    square = cov_ref[0:rows, own]
    on_diagonal = lax.broadcasted_iota(jnp.int32, (rows, rows), 0) == lax.broadcasted_iota(
        jnp.int32, (rows, rows), 1
    )
    own_trace = jnp.sum(jnp.where(on_diagonal, square, 0.0), axis=(0, 1), keepdims=True)
    traces[me] = jnp.broadcast_to(own_trace, traces.shape[1:])
    send(traces, tr_send, tr_recv)

    def subspace_round(step, carry):
        now, later = lax.rem(step, 2), lax.rem(step + 1, 2)
        arrive(vectors.at[now], vec_send.at[now], vec_recv.at[now])
        block = whole(vectors.at[now])
        moved = complex_rows(dot_nt(block, cov_ref[...]), count, rows)
        factor = inverse_factor(*hermitian_parts(dot_nt(block, block), count), count)
        factor_ref[...] = factor
        vectors[later, me] = dot_nn(factor, moved)
        send(vectors.at[later], vec_send.at[later], vec_recv.at[later])
        return carry

    lax.fori_loop(0, SUB_ITERS, subspace_round, 0)
    last, after = (SUB_ITERS - 1) % 2, SUB_ITERS % 2
    flag = flag_ref[...].astype(jnp.float32)
    basis = dot_nn(factor_ref[...], whole(vectors.at[last])) * flag
    basis_ref[...] = basis
    arrive(vectors.at[after], vec_send.at[after], vec_recv.at[after])
    image = whole(vectors.at[after]) * flag
    inner = embed(*hermitian_parts(dot_nt(image, basis), count))
    wide_ref[0 : 2 * count, :] = image - 0.5 * dot_nn(inner, basis)
    wide_ref[2 * count :, :] = basis
    own_basis = basis_ref[:, own]
    own_wide = wide_ref[0 : 2 * count, own]
    left_real = jnp.concatenate([own_basis, own_wide], 0)
    left_imag = jnp.concatenate(
        [own_basis[count:], -own_basis[:count], own_wide[count:], -own_wide[:count]], 0
    )
    left = jnp.concatenate([left_real.T, left_imag.T], 0)

    @pl.loop(0, peers)
    def _(j):
        part = pl.ds(pl.multiple_of(j * rows, rows), rows)
        projected = cov_ref[:, part] - dot_nn(left, wide_ref[:, part])
        high, low = split_halves(projected)
        high_ref[:, part] = high
        low_ref[:, part] = low

    arrive(traces, tr_send, tr_recv)
    trace = traces[0, 0:1, 0:1]
    for j in range(1, peers):
        trace = trace + traces[j, 0:1, 0:1]
    load = diagonal_loading * trace / antennas

    def inner_product(a, b):
        each = jnp.sum(a * b, axis=1, keepdims=True)
        return each[:beams] + each[beams:]

    def both(each):
        return jnp.concatenate([each, each], 0)

    steering = steer_ref[...]
    x_ref[...] = jnp.zeros_like(steering)
    r_ref[...] = steering
    p_ref[...] = steering

    def cg_step(step, norm):
        slot = lax.rem(step, 2)
        direction = p_ref[...]
        high, low = split_halves(direction)
        top = dot_nt16(jnp.concatenate([high, low], 0), high_ref[...])
        product = top[: 2 * beams] + top[2 * beams :] + dot_nt16(high, low_ref[...])
        mapped[slot, me] = complex_rows(product, beams, rows)
        send(mapped.at[slot], map_send.at[slot], map_recv.at[slot])
        arrive(mapped.at[slot], map_send.at[slot], map_recv.at[slot])
        combined = whole(mapped.at[slot]) + load * direction
        alpha = norm / inner_product(direction, combined)
        alpha_rows = both(alpha)
        x_ref[...] = x_ref[...] + alpha_rows * direction
        residual = r_ref[...] - alpha_rows * combined
        r_ref[...] = residual
        new_norm = inner_product(residual, residual)
        p_ref[...] = residual + both(new_norm / norm) * direction
        return new_norm

    lax.fori_loop(0, CG_ITERS, cg_step, inner_product(steering, steering))
    response = both(inner_product(steer_ref[...], x_ref[...]))
    out_ref[...] = antennas * x_ref[:, own] / response


def beam_weights(covariance, rfi_flags, beam_steer_index, start_columns):
    peers = lax.axis_size("tile")
    _, _, rows, antennas = covariance.shape
    beams = beam_steer_index.shape[1]
    count = start_columns.shape[1]
    steering = steering_table(beam_steer_index[0], antennas).reshape(2 * beams, antennas)
    f32, b16 = jnp.float32, jnp.bfloat16
    dma = pltpu.SemaphoreType.DMA
    out = pl.pallas_call(
        functools.partial(tail_kernel, peers),
        out_shape=jax.ShapeDtypeStruct((2 * beams, rows), f32),
        in_specs=[pl.BlockSpec(memory_space=pltpu.VMEM)] * 4,
        out_specs=pl.BlockSpec(memory_space=pltpu.VMEM),
        scratch_shapes=[
            pltpu.VMEM((2, peers, 2 * count, rows), f32),
            pltpu.VMEM((2, peers, 2 * beams, rows), f32),
            pltpu.VMEM((peers, 8, 128), f32),
            pltpu.VMEM((2 * count, 2 * count), f32),
            pltpu.VMEM((2 * count, antennas), f32),
            pltpu.VMEM((4 * count, antennas), f32),
            pltpu.VMEM((2 * rows, antennas), b16),
            pltpu.VMEM((2 * rows, antennas), b16),
            pltpu.VMEM((2 * beams, antennas), f32),
            pltpu.VMEM((2 * beams, antennas), f32),
            pltpu.VMEM((2 * beams, antennas), f32),
            dma((2, peers)),
            dma((2, peers)),
            dma((2, peers)),
            dma((2, peers)),
            dma((peers,)),
            dma((peers,)),
        ],
        compiler_params=pltpu.CompilerParams(
            collective_id=0, has_side_effects=True, vmem_limit_bytes=48 * 1024 * 1024
        ),
    )(
        covariance.reshape(2 * rows, antennas),
        start_columns,
        rfi_flags.reshape(1, 1),
        steering,
    )
    return jnp.swapaxes(out.reshape(2, beams, rows), 0, 1)[None]


def shards(voltages, rfi_flags, beam_steer_index, start_columns):
    covariance = channel_covariance(voltages)
    weights = beam_weights(covariance, rfi_flags, beam_steer_index, start_columns)
    return (covariance, weights)


def solution(mesh):
    in_specs = (P(None, None, "tile", "chan"), P("chan"), P("chan", None), P("chan", None))
    out_specs = (P("chan", None, "tile", None), P("chan", None, None, "tile"))
    return jax.shard_map(shards, mesh=mesh, in_specs=in_specs, out_specs=out_specs, check_vma=False)
```

```python
import functools
import math

import jax
import jax.numpy as jnp
from jax import lax
from jax.experimental import pallas as pl
from jax.experimental.pallas import tpu as pltpu
from jax.sharding import PartitionSpec as P

SUB_ITERS = 4
CG_ITERS = 12


diagonal_loading = 0.1
highest = lax.Precision.HIGHEST
MESH = pl.DeviceIdType.MESH


def steering_table(beam_entries, element_total):
    element_index = jnp.arange(element_total, dtype=jnp.int32)
    steer_phases = (beam_entries[..., None] * element_index % element_total).astype(
        jnp.float32
    ) * (2.0 * math.pi / element_total)
    return jnp.stack([jnp.cos(steer_phases), jnp.sin(steer_phases)], axis=0)


def dot_nt(a, b):
    return lax.dot_general(
        a, b, (((1,), (1,)), ((), ())), precision=highest, preferred_element_type=jnp.float32
    )


def dot_nn(a, b):
    return lax.dot_general(
        a, b, (((1,), (0,)), ((), ())), precision=highest, preferred_element_type=jnp.float32
    )


def dot16(a, b):
    return jnp.dot(a, b, preferred_element_type=jnp.float32)


def split_thirds(values):
    high = values.astype(jnp.bfloat16)
    rest = values - high.astype(jnp.float32)
    middle = rest.astype(jnp.bfloat16)
    low = (rest - middle.astype(jnp.float32)).astype(jnp.bfloat16)
    return high, middle, low


def split_halves(values):
    high = values.astype(jnp.bfloat16)
    low = (values - high.astype(jnp.float32)).astype(jnp.bfloat16)
    return high, low


def complex_rows(product, count, rows):
    real = product[:count, :rows] - product[count:, rows:]
    imag = product[count:, :rows] + product[:count, rows:]
    return jnp.concatenate([real, imag], 0)


def embed(real, imag):
    return jnp.concatenate(
        [jnp.concatenate([real, -imag], 1), jnp.concatenate([imag, real], 1)], 0
    )


def hermitian_parts(product, count):
    real = product[:count, :count] + product[count:, count:]
    imag = product[count:, :count] - product[:count, count:]
    return real, imag


def inverse_factor(gram_real, gram_imag, count):
    row_id = lax.broadcasted_iota(jnp.int32, (count, count), 0)
    col_id = lax.broadcasted_iota(jnp.int32, (count, count), 1)
    eye = (row_id == col_id).astype(jnp.float32)
    system = jnp.concatenate([gram_real, gram_imag, eye, jnp.zeros_like(eye)], 1)
    below = lax.broadcasted_iota(jnp.int32, (count, 1), 0)
    lane = lax.broadcasted_iota(jnp.int32, (1, 4 * count), 1)
    first_half = lax.rem(lane, 2 * count) < count
    for k in range(count):
        row = system[k : k + 1, :]
        fore = pltpu.roll(row, 3 * count, 1)
        back = pltpu.roll(row, count, 1)
        turned = jnp.where(first_half, -fore, back)
        scale = jnp.where(below > k, 1.0 / row[:, k : k + 1], 0.0)
        factor_real = system[:, k : k + 1] * scale
        factor_imag = system[:, count + k : count + k + 1] * scale
        system = system - factor_real * row - factor_imag * turned
    pivots = jnp.sum(system[:, :count] * eye, axis=1, keepdims=True)
    system = system * lax.rsqrt(pivots)
    return embed(system[:, 2 * count : 3 * count], system[:, 3 * count :])


def ring_place(position, peers):
    half = peers // 2
    return jnp.where(position < half, 2 * position, 2 * (peers - 1 - position) + 1)


def covariance_kernel(
    peers, groups, volt_ref, cov_ref, shards_ref, left_ref, local_sem, turn_send, turn_recv, ring_send, ring_recv
):
    me = lax.axis_index("tile")
    chan = lax.axis_index("chan")
    _, _, depth, width = volt_ref.shape
    rows = cov_ref.shape[0] // 2
    antennas = cov_ref.shape[1]
    half = peers // 2
    own = pl.ds(pl.multiple_of(me * rows, rows), rows)
    odd = lax.rem(me, 2)
    position = jnp.where(odd == 0, me // 2, peers - 1 - me // 2)

    def tile_at(offset):
        return ring_place(lax.rem(position + offset + peers, peers), peers)

    right, left = tile_at(1), tile_at(-1)

    barrier = pltpu.get_barrier_semaphore()
    for k in range(1, groups):
        pl.semaphore_signal(
            barrier, inc=1, device_id={"chan": lax.rem(chan + k, groups)}, device_id_type=MESH
        )
    for neighbour in (left, right):
        pl.semaphore_signal(barrier, inc=1, device_id={"tile": neighbour}, device_id_type=MESH)
    pl.semaphore_wait(barrier, groups + 1)

    def piece(tile, source):
        lanes = pl.ds(pl.multiple_of(source * width, width), width)
        return shards_ref.at[tile, :, :, lanes]

    def turn_copy(k):
        return pltpu.make_async_remote_copy(
            src_ref=volt_ref.at[lax.rem(chan + k, groups)],
            dst_ref=piece(me, chan),
            send_sem=turn_send.at[k],
            recv_sem=turn_recv.at[k],
            device_id={"chan": lax.rem(chan + k, groups)},
            device_id_type=MESH,
        )

    def turn_arrival(k):
        source = lax.rem(chan - k + groups, groups)
        return pltpu.make_async_remote_copy(
            src_ref=volt_ref.at[chan],
            dst_ref=piece(me, source),
            send_sem=turn_send.at[k],
            recv_sem=turn_recv.at[k],
            device_id={"chan": lax.rem(chan + k, groups)},
            device_id_type=MESH,
        )

    def hops(way, k):
        longer = 0 if k < groups // 2 else 1
        return half if way == longer else half - 1

    def ring_copy(way, hop, k, arriving=False):
        step = 1 if way == 0 else -1
        tile = tile_at(-step * (hop + 1 if arriving else hop))
        part = piece(tile, lax.rem(chan - k + groups, groups))
        return pltpu.make_async_remote_copy(
            src_ref=part,
            dst_ref=part,
            send_sem=ring_send.at[way, hop, k],
            recv_sem=ring_recv.at[way, hop, k],
            device_id={"tile": right if way == 0 else left},
            device_id_type=MESH,
        )

    def add_shard(tile, first=False, scale=None):
        real, imag = shards_ref[tile, 0, :, own], shards_ref[tile, 1, :, own]
        left_ref[...] = jnp.concatenate(
            [jnp.concatenate([real, imag], 1), jnp.concatenate([imag, -real], 1)], 0
        ).T

        @pl.loop(0, peers)
        def _(j):
            part = pl.ds(pl.multiple_of(j * rows, rows), rows)
            right_part = jnp.concatenate(
                [shards_ref[tile, 0, :, part], shards_ref[tile, 1, :, part]], 0
            )
            term = jnp.dot(left_ref[...], right_part, preferred_element_type=jnp.float32)
            if not first:
                term = term + cov_ref[:, part]
            if scale is not None:
                term = term * scale
            cov_ref[:, part] = term

    local = pltpu.make_async_copy(volt_ref.at[chan], piece(me, chan), local_sem)
    for k in range(1, groups):
        turn_copy(k).start()
    local.start()
    for k in range(groups):
        if k == 0:
            local.wait()
        else:
            turn_arrival(k).wait_recv()
        for way in range(2):
            ring_copy(way, 0, k).start()
    add_shard(me, first=True)
    for hop in range(half):
        for k in range(groups):
            for way in range(2):
                if hop < hops(way, k):
                    ring_copy(way, hop, k, arriving=True).wait_recv()
                    if hop + 1 < hops(way, k):
                        ring_copy(way, hop + 1, k).start()
        if hop + 1 < half:
            add_shard(tile_at(-hop - 1))
            add_shard(tile_at(hop + 1))
        else:
            add_shard(tile_at(half), scale=1.0 / (depth * peers))
    for k in range(1, groups):
        turn_copy(k).wait_send()
    for k in range(groups):
        for way in range(2):
            for hop in range(hops(way, k)):
                ring_copy(way, hop, k).wait_send()


def channel_covariance(voltages):
    peers, groups = lax.axis_size("tile"), lax.axis_size("chan")
    _, _, depth, width = voltages.shape
    antennas = width * groups
    rows = antennas // peers
    dma = pltpu.SemaphoreType.DMA
    out = pl.pallas_call(
        functools.partial(covariance_kernel, peers, groups),
        out_shape=jax.ShapeDtypeStruct((2 * rows, antennas), jnp.float32),
        in_specs=[pl.BlockSpec(memory_space=pl.ANY)],
        out_specs=pl.BlockSpec(memory_space=pltpu.VMEM),
        scratch_shapes=[
            pltpu.VMEM((peers, 2, depth, antennas), voltages.dtype),
            pltpu.VMEM((2 * rows, 2 * depth), voltages.dtype),
            dma(()),
            dma((groups,)),
            dma((groups,)),
            dma((2, peers // 2, groups)),
            dma((2, peers // 2, groups)),
        ],
        compiler_params=pltpu.CompilerParams(
            collective_id=1, has_side_effects=True, vmem_limit_bytes=40 * 1024 * 1024
        ),
    )(voltages)
    return out.reshape(1, 2, rows, antennas)


def tail_kernel(
    peers,
    cov_ref,
    columns_ref,
    flag_ref,
    steer_ref,
    out_ref,
    vectors,
    mapped,
    traces,
    factor_ref,
    basis_ref,
    wide_ref,
    parts_ref,
    x_ref,
    r_ref,
    p_ref,
    vec_send,
    vec_recv,
    map_send,
    map_recv,
    tr_send,
    tr_recv,
):
    me = lax.axis_index("tile")
    rows = cov_ref.shape[0] // 2
    antennas = cov_ref.shape[1]
    count = columns_ref.shape[0]
    beams = steer_ref.shape[0] // 2
    own = pl.ds(pl.multiple_of(me * rows, rows), rows)

    barrier = pltpu.get_barrier_semaphore()
    for k in range(1, peers):
        pl.semaphore_signal(
            barrier, inc=1, device_id={"tile": lax.rem(me + k, peers)}, device_id_type=MESH
        )
    pl.semaphore_wait(barrier, peers - 1)

    def send(block, send_sem, recv_sem):
        for k in range(1, peers):
            pltpu.make_async_remote_copy(
                src_ref=block.at[me],
                dst_ref=block.at[me],
                send_sem=send_sem.at[k],
                recv_sem=recv_sem.at[k],
                device_id={"tile": lax.rem(me + k, peers)},
                device_id_type=MESH,
            ).start()

    def arrive(block, send_sem, recv_sem):
        for k in range(1, peers):
            source = lax.rem(me - k + peers, peers)
            copy = pltpu.make_async_remote_copy(
                src_ref=block.at[me],
                dst_ref=block.at[source],
                send_sem=send_sem.at[k],
                recv_sem=recv_sem.at[k],
                device_id={"tile": lax.rem(me + k, peers)},
                device_id_type=MESH,
            )
            copy.wait_send()
            copy.wait_recv()

    def whole(block):
        return jnp.concatenate([block[j] for j in range(peers)], 1)

    @pl.loop(0, peers)
    def _(j):
        part = pl.ds(pl.multiple_of(j * rows, rows), rows)
        thirds = split_thirds(cov_ref[:, part].T)
        for third, values in enumerate(thirds):
            parts_ref[third, part, :] = values

    hot = jnp.where(
        lax.broadcasted_iota(jnp.int32, (count, antennas), 1) == columns_ref[...], 1.0, 0.0
    ).astype(jnp.bfloat16)
    picked = dot16(hot, parts_ref[0]) + (dot16(hot, parts_ref[1]) + dot16(hot, parts_ref[2]))
    vectors[0, me] = jnp.concatenate([picked[:, :rows], picked[:, rows:]], 0)
    send(vectors.at[0], vec_send.at[0], vec_recv.at[0])

    square = cov_ref[0:rows, own]
    on_diagonal = lax.broadcasted_iota(jnp.int32, (rows, rows), 0) == lax.broadcasted_iota(
        jnp.int32, (rows, rows), 1
    )
    own_trace = jnp.sum(jnp.where(on_diagonal, square, 0.0), axis=(0, 1), keepdims=True)
    traces[me] = jnp.broadcast_to(own_trace, traces.shape[1:])
    send(traces, tr_send, tr_recv)

    def subspace_round(step, carry):
        now, later = lax.rem(step, 2), lax.rem(step + 1, 2)
        arrive(vectors.at[now], vec_send.at[now], vec_recv.at[now])
        block = whole(vectors.at[now])
        size = 2 * count
        high, middle, low = split_thirds(block)
        top = dot16(jnp.concatenate([high, middle, low], 0), parts_ref[0])
        mid = dot16(jnp.concatenate([high, middle], 0), parts_ref[1])
        small = top[2 * size :] + mid[size:] + dot16(high, parts_ref[2])
        moved = complex_rows(top[:size] + (top[size : 2 * size] + mid[:size] + small), count, rows)
        factor = inverse_factor(*hermitian_parts(dot_nt(block, block), count), count)
        factor_ref[...] = factor
        vectors[later, me] = dot_nn(factor, moved)
        send(vectors.at[later], vec_send.at[later], vec_recv.at[later])
        return carry

    lax.fori_loop(0, SUB_ITERS, subspace_round, 0)
    last, after = (SUB_ITERS - 1) % 2, SUB_ITERS % 2
    flag = flag_ref[...].astype(jnp.float32)
    basis = dot_nn(factor_ref[...], whole(vectors.at[last])) * flag
    basis_ref[...] = basis
    arrive(vectors.at[after], vec_send.at[after], vec_recv.at[after])
    image = whole(vectors.at[after]) * flag
    inner = embed(*hermitian_parts(dot_nt(image, basis), count))
    wide_ref[0 : 2 * count, :] = image - 0.5 * dot_nn(inner, basis)
    wide_ref[2 * count :, :] = basis
    own_basis = basis_ref[:, own]
    own_wide = wide_ref[0 : 2 * count, own]
    left_real = jnp.concatenate([own_basis, own_wide], 0)
    left_imag = jnp.concatenate(
        [own_basis[count:], -own_basis[:count], own_wide[count:], -own_wide[:count]], 0
    )
    left = jnp.concatenate([left_real.T, left_imag.T], 0)

    @pl.loop(0, peers)
    def _(j):
        part = pl.ds(pl.multiple_of(j * rows, rows), rows)
        projected = cov_ref[:, part] - dot_nn(left, wide_ref[:, part])
        high, low = split_halves(projected.T)
        parts_ref[0, part, :] = high
        parts_ref[1, part, :] = low

    arrive(traces, tr_send, tr_recv)
    trace = traces[0, 0:1, 0:1]
    for j in range(1, peers):
        trace = trace + traces[j, 0:1, 0:1]
    load = diagonal_loading * trace / antennas

    def inner_product(a, b):
        each = jnp.sum(a * b, axis=1, keepdims=True)
        return each[:beams] + each[beams:]

    def both(each):
        return jnp.concatenate([each, each], 0)

    steering = steer_ref[...]
    x_ref[...] = jnp.zeros_like(steering)
    r_ref[...] = steering
    p_ref[...] = steering

    def cg_step(step, norm):
        slot = lax.rem(step, 2)
        direction = p_ref[...]
        high, low = split_halves(direction)
        top = dot16(jnp.concatenate([high, low], 0), parts_ref[0])
        product = top[: 2 * beams] + top[2 * beams :] + dot16(high, parts_ref[1])
        mapped[slot, me] = complex_rows(product, beams, rows)
        send(mapped.at[slot], map_send.at[slot], map_recv.at[slot])
        arrive(mapped.at[slot], map_send.at[slot], map_recv.at[slot])
        combined = whole(mapped.at[slot]) + load * direction
        alpha = norm / inner_product(direction, combined)
        alpha_rows = both(alpha)
        x_ref[...] = x_ref[...] + alpha_rows * direction
        residual = r_ref[...] - alpha_rows * combined
        r_ref[...] = residual
        new_norm = inner_product(residual, residual)
        p_ref[...] = residual + both(new_norm / norm) * direction
        return new_norm

    lax.fori_loop(0, CG_ITERS, cg_step, inner_product(steering, steering))
    response = both(inner_product(steer_ref[...], x_ref[...]))
    out_ref[...] = antennas * x_ref[:, own] / response


def beam_weights(covariance, rfi_flags, beam_steer_index, start_columns):
    peers = lax.axis_size("tile")
    _, _, rows, antennas = covariance.shape
    beams = beam_steer_index.shape[1]
    count = start_columns.shape[1]
    steering = steering_table(beam_steer_index[0], antennas).reshape(2 * beams, antennas)
    f32, b16 = jnp.float32, jnp.bfloat16
    dma = pltpu.SemaphoreType.DMA
    out = pl.pallas_call(
        functools.partial(tail_kernel, peers),
        out_shape=jax.ShapeDtypeStruct((2 * beams, rows), f32),
        in_specs=[pl.BlockSpec(memory_space=pltpu.VMEM)] * 4,
        out_specs=pl.BlockSpec(memory_space=pltpu.VMEM),
        scratch_shapes=[
            pltpu.VMEM((2, peers, 2 * count, rows), f32),
            pltpu.VMEM((2, peers, 2 * beams, rows), f32),
            pltpu.VMEM((peers, 8, 128), f32),
            pltpu.VMEM((2 * count, 2 * count), f32),
            pltpu.VMEM((2 * count, antennas), f32),
            pltpu.VMEM((4 * count, antennas), f32),
            pltpu.VMEM((3, antennas, 2 * rows), b16),
            pltpu.VMEM((2 * beams, antennas), f32),
            pltpu.VMEM((2 * beams, antennas), f32),
            pltpu.VMEM((2 * beams, antennas), f32),
            dma((2, peers)),
            dma((2, peers)),
            dma((2, peers)),
            dma((2, peers)),
            dma((peers,)),
            dma((peers,)),
        ],
        compiler_params=pltpu.CompilerParams(
            collective_id=0, has_side_effects=True, vmem_limit_bytes=48 * 1024 * 1024
        ),
    )(
        covariance.reshape(2 * rows, antennas),
        start_columns.reshape(count, 1),
        rfi_flags.reshape(1, 1),
        steering,
    )
    return jnp.swapaxes(out.reshape(2, beams, rows), 0, 1)[None]


def shards(voltages, rfi_flags, beam_steer_index, start_columns):
    covariance = channel_covariance(voltages)
    weights = beam_weights(covariance, rfi_flags, beam_steer_index, start_columns)
    return (covariance, weights)


def solution(mesh):
    in_specs = (P(None, None, "tile", "chan"), P("chan"), P("chan", None), P("chan", None))
    out_specs = (P("chan", None, "tile", None), P("chan", None, None, "tile"))
    return jax.shard_map(shards, mesh=mesh, in_specs=in_specs, out_specs=out_specs, check_vma=False)
```

```python
import functools
import math

import jax
import jax.numpy as jnp
from jax import lax
from jax.experimental import pallas as pl
from jax.experimental.pallas import tpu as pltpu
from jax.sharding import PartitionSpec as P

SUB_ITERS = 4
CG_ITERS = 12


diagonal_loading = 0.1
highest = lax.Precision.HIGHEST
MESH = pl.DeviceIdType.MESH


def steering_table(beam_entries, element_total):
    element_index = jnp.arange(element_total, dtype=jnp.int32)
    steer_phases = (beam_entries[..., None] * element_index % element_total).astype(
        jnp.float32
    ) * (2.0 * math.pi / element_total)
    return jnp.stack([jnp.cos(steer_phases), jnp.sin(steer_phases)], axis=0)


def dot_nt(a, b):
    return lax.dot_general(
        a, b, (((1,), (1,)), ((), ())), precision=highest, preferred_element_type=jnp.float32
    )


def dot_nn(a, b):
    return lax.dot_general(
        a, b, (((1,), (0,)), ((), ())), precision=highest, preferred_element_type=jnp.float32
    )


def dot16(a, b):
    return jnp.dot(a, b, preferred_element_type=jnp.float32)


def split_thirds(values):
    high = values.astype(jnp.bfloat16)
    rest = values - high.astype(jnp.float32)
    middle = rest.astype(jnp.bfloat16)
    low = (rest - middle.astype(jnp.float32)).astype(jnp.bfloat16)
    return high, middle, low


def split_halves(values):
    high = values.astype(jnp.bfloat16)
    low = (values - high.astype(jnp.float32)).astype(jnp.bfloat16)
    return high, low


def complex_rows(product, count, rows):
    real = product[:count, :rows] - product[count:, rows:]
    imag = product[count:, :rows] + product[:count, rows:]
    return jnp.concatenate([real, imag], 0)


def embed(real, imag):
    return jnp.concatenate(
        [jnp.concatenate([real, -imag], 1), jnp.concatenate([imag, real], 1)], 0
    )


def hermitian_parts(product, count):
    real = product[:count, :count] + product[count:, count:]
    imag = product[count:, :count] - product[:count, count:]
    return real, imag


def inverse_factor(gram_real, gram_imag, count):
    row_id = lax.broadcasted_iota(jnp.int32, (count, count), 0)
    col_id = lax.broadcasted_iota(jnp.int32, (count, count), 1)
    eye = (row_id == col_id).astype(jnp.float32)
    system = jnp.concatenate([gram_real, gram_imag, eye, jnp.zeros_like(eye)], 1)
    below = lax.broadcasted_iota(jnp.int32, (count, 1), 0)
    lane = lax.broadcasted_iota(jnp.int32, (1, 4 * count), 1)
    first_half = lax.rem(lane, 2 * count) < count
    for k in range(count):
        row = system[k : k + 1, :]
        fore = pltpu.roll(row, 3 * count, 1)
        back = pltpu.roll(row, count, 1)
        turned = jnp.where(first_half, -fore, back)
        scale = jnp.where(below > k, 1.0 / row[:, k : k + 1], 0.0)
        factor_real = system[:, k : k + 1] * scale
        factor_imag = system[:, count + k : count + k + 1] * scale
        system = system - factor_real * row - factor_imag * turned
    pivots = jnp.sum(system[:, :count] * eye, axis=1, keepdims=True)
    system = system * lax.rsqrt(pivots)
    return embed(system[:, 2 * count : 3 * count], system[:, 3 * count :])


def ring_place(position, peers):
    half = peers // 2
    return jnp.where(position < half, 2 * position, 2 * (peers - 1 - position) + 1)


def covariance_kernel(
    peers, groups, volt_ref, cov_ref, shards_ref, left_ref, local_sem, turn_send, turn_recv, ring_send, ring_recv
):
    me = lax.axis_index("tile")
    chan = lax.axis_index("chan")
    _, _, depth, width = volt_ref.shape
    rows = cov_ref.shape[0] // 2
    antennas = cov_ref.shape[1]
    half = peers // 2
    own = pl.ds(pl.multiple_of(me * rows, rows), rows)
    odd = lax.rem(me, 2)
    position = jnp.where(odd == 0, me // 2, peers - 1 - me // 2)

    def tile_at(offset):
        return ring_place(lax.rem(position + offset + peers, peers), peers)

    right, left = tile_at(1), tile_at(-1)

    barrier = pltpu.get_barrier_semaphore()
    for k in range(1, groups):
        pl.semaphore_signal(
            barrier, inc=1, device_id={"chan": lax.rem(chan + k, groups)}, device_id_type=MESH
        )
    for neighbour in (left, right):
        pl.semaphore_signal(barrier, inc=1, device_id={"tile": neighbour}, device_id_type=MESH)
    pl.semaphore_wait(barrier, groups + 1)

    def piece(tile, source):
        lanes = pl.ds(pl.multiple_of(source * width, width), width)
        return shards_ref.at[tile, :, :, lanes]

    def turn_copy(k):
        return pltpu.make_async_remote_copy(
            src_ref=volt_ref.at[lax.rem(chan + k, groups)],
            dst_ref=piece(me, chan),
            send_sem=turn_send.at[k],
            recv_sem=turn_recv.at[k],
            device_id={"chan": lax.rem(chan + k, groups)},
            device_id_type=MESH,
        )

    def turn_arrival(k):
        source = lax.rem(chan - k + groups, groups)
        return pltpu.make_async_remote_copy(
            src_ref=volt_ref.at[chan],
            dst_ref=piece(me, source),
            send_sem=turn_send.at[k],
            recv_sem=turn_recv.at[k],
            device_id={"chan": lax.rem(chan + k, groups)},
            device_id_type=MESH,
        )

    def hops(way, k):
        longer = 0 if k < groups // 2 else 1
        return half if way == longer else half - 1

    def ring_copy(way, hop, k, arriving=False):
        step = 1 if way == 0 else -1
        tile = tile_at(-step * (hop + 1 if arriving else hop))
        part = piece(tile, lax.rem(chan - k + groups, groups))
        return pltpu.make_async_remote_copy(
            src_ref=part,
            dst_ref=part,
            send_sem=ring_send.at[way, hop, k],
            recv_sem=ring_recv.at[way, hop, k],
            device_id={"tile": right if way == 0 else left},
            device_id_type=MESH,
        )

    def add_shard(tile, first=False, scale=None):
        real, imag = shards_ref[tile, 0, :, own], shards_ref[tile, 1, :, own]
        left_ref[...] = jnp.concatenate(
            [jnp.concatenate([real, imag], 1), jnp.concatenate([imag, -real], 1)], 0
        ).T

        @pl.loop(0, peers)
        def _(j):
            part = pl.ds(pl.multiple_of(j * rows, rows), rows)
            right_part = jnp.concatenate(
                [shards_ref[tile, 0, :, part], shards_ref[tile, 1, :, part]], 0
            )
            term = jnp.dot(left_ref[...], right_part, preferred_element_type=jnp.float32)
            if not first:
                term = term + cov_ref[:, part]
            if scale is not None:
                term = term * scale
            cov_ref[:, part] = term

    local = pltpu.make_async_copy(volt_ref.at[chan], piece(me, chan), local_sem)
    for k in range(1, groups):
        turn_copy(k).start()
    local.start()
    for k in range(groups):
        if k == 0:
            local.wait()
        else:
            turn_arrival(k).wait_recv()
        for way in range(2):
            ring_copy(way, 0, k).start()
    add_shard(me, first=True)
    for hop in range(half):
        for k in range(groups):
            for way in range(2):
                if hop < hops(way, k):
                    ring_copy(way, hop, k, arriving=True).wait_recv()
                    if hop + 1 < hops(way, k):
                        ring_copy(way, hop + 1, k).start()
        if hop + 1 < half:
            add_shard(tile_at(-hop - 1))
            add_shard(tile_at(hop + 1))
        else:
            add_shard(tile_at(half), scale=1.0 / (depth * peers))
    for k in range(1, groups):
        turn_copy(k).wait_send()
    for k in range(groups):
        for way in range(2):
            for hop in range(hops(way, k)):
                ring_copy(way, hop, k).wait_send()


def channel_covariance(voltages):
    peers, groups = lax.axis_size("tile"), lax.axis_size("chan")
    _, _, depth, width = voltages.shape
    antennas = width * groups
    rows = antennas // peers
    dma = pltpu.SemaphoreType.DMA
    out = pl.pallas_call(
        functools.partial(covariance_kernel, peers, groups),
        out_shape=jax.ShapeDtypeStruct((2 * rows, antennas), jnp.float32),
        in_specs=[pl.BlockSpec(memory_space=pl.ANY)],
        out_specs=pl.BlockSpec(memory_space=pltpu.VMEM),
        scratch_shapes=[
            pltpu.VMEM((peers, 2, depth, antennas), voltages.dtype),
            pltpu.VMEM((2 * rows, 2 * depth), voltages.dtype),
            dma(()),
            dma((groups,)),
            dma((groups,)),
            dma((2, peers // 2, groups)),
            dma((2, peers // 2, groups)),
        ],
        compiler_params=pltpu.CompilerParams(
            collective_id=1, has_side_effects=True, vmem_limit_bytes=40 * 1024 * 1024
        ),
    )(voltages)
    return out.reshape(1, 2, rows, antennas)


def tail_kernel(
    peers,
    cov_ref,
    columns_ref,
    flag_ref,
    steer_ref,
    out_ref,
    vectors,
    mapped,
    traces,
    factor_ref,
    basis_ref,
    wide_ref,
    parts_ref,
    x_ref,
    r_ref,
    p_ref,
    vec_send,
    vec_recv,
    map_send,
    map_recv,
    tr_send,
    tr_recv,
):
    me = lax.axis_index("tile")
    rows = cov_ref.shape[0] // 2
    antennas = cov_ref.shape[1]
    count = columns_ref.shape[0]
    beams = steer_ref.shape[0] // 2
    own = pl.ds(pl.multiple_of(me * rows, rows), rows)

    barrier = pltpu.get_barrier_semaphore()
    for k in range(1, peers):
        pl.semaphore_signal(
            barrier, inc=1, device_id={"tile": lax.rem(me + k, peers)}, device_id_type=MESH
        )
    pl.semaphore_wait(barrier, peers - 1)

    def send(block, send_sem, recv_sem):
        for k in range(1, peers):
            pltpu.make_async_remote_copy(
                src_ref=block.at[me],
                dst_ref=block.at[me],
                send_sem=send_sem.at[k],
                recv_sem=recv_sem.at[k],
                device_id={"tile": lax.rem(me + k, peers)},
                device_id_type=MESH,
            ).start()

    def arrive(block, send_sem, recv_sem):
        for k in range(1, peers):
            source = lax.rem(me - k + peers, peers)
            copy = pltpu.make_async_remote_copy(
                src_ref=block.at[me],
                dst_ref=block.at[source],
                send_sem=send_sem.at[k],
                recv_sem=recv_sem.at[k],
                device_id={"tile": lax.rem(me + k, peers)},
                device_id_type=MESH,
            )
            copy.wait_send()
            copy.wait_recv()

    half = peers // 2
    line, side = me // 2, lax.rem(me, 2)
    partner = 2 * line + 1 - side

    def hand_over(block, tile, landed, target, send_sem, recv_sem, index):
        return pltpu.make_async_remote_copy(
            src_ref=block.at[tile],
            dst_ref=block.at[landed],
            send_sem=send_sem.at[index],
            recv_sem=recv_sem.at[index],
            device_id={"tile": target},
            device_id_type=MESH,
        )

    def along(k):
        return 2 * lax.rem(line + k + half, half) + side

    def send_staged(block, send_sem, recv_sem):
        for k in range(1, half):
            hand_over(block, me, me, along(k), send_sem, recv_sem, k).start()
        hand_over(block, me, me, partner, send_sem, recv_sem, half).start()

    def arrive_staged(block, send_sem, recv_sem):
        for k in range(1, half):
            source = along(-k)
            hand_over(block, me, source, along(k), send_sem, recv_sem, k).wait_recv()
            hand_over(block, source, source, partner, send_sem, recv_sem, half + k).start()
        for k in range(half):
            source = along(-k)
            across = 2 * (source // 2) + 1 - side
            hand_over(block, source, across, partner, send_sem, recv_sem, half + k).wait_recv()
            hand_over(block, source, source, partner, send_sem, recv_sem, half + k).wait_send()
        for k in range(1, half):
            hand_over(block, me, me, along(k), send_sem, recv_sem, k).wait_send()

    def whole(block):
        return jnp.concatenate([block[j] for j in range(peers)], 1)

    @pl.loop(0, peers)
    def _(j):
        part = pl.ds(pl.multiple_of(j * rows, rows), rows)
        thirds = split_thirds(cov_ref[:, part].T)
        for third, values in enumerate(thirds):
            parts_ref[third, part, :] = values

    hot = jnp.where(
        lax.broadcasted_iota(jnp.int32, (count, antennas), 1) == columns_ref[...], 1.0, 0.0
    ).astype(jnp.bfloat16)
    picked = dot16(hot, parts_ref[0]) + (dot16(hot, parts_ref[1]) + dot16(hot, parts_ref[2]))
    vectors[0, me] = jnp.concatenate([picked[:, :rows], picked[:, rows:]], 0)
    send_staged(vectors.at[0], vec_send.at[0], vec_recv.at[0])

    square = cov_ref[0:rows, own]
    on_diagonal = lax.broadcasted_iota(jnp.int32, (rows, rows), 0) == lax.broadcasted_iota(
        jnp.int32, (rows, rows), 1
    )
    own_trace = jnp.sum(jnp.where(on_diagonal, square, 0.0), axis=(0, 1), keepdims=True)
    traces[me] = jnp.broadcast_to(own_trace, traces.shape[1:])
    send(traces, tr_send, tr_recv)

    def subspace_round(step, carry):
        now, later = lax.rem(step, 2), lax.rem(step + 1, 2)
        arrive_staged(vectors.at[now], vec_send.at[now], vec_recv.at[now])
        block = whole(vectors.at[now])
        size = 2 * count
        high, middle, low = split_thirds(block)
        top = dot16(jnp.concatenate([high, middle, low], 0), parts_ref[0])
        mid = dot16(jnp.concatenate([high, middle], 0), parts_ref[1])
        small = top[2 * size :] + mid[size:] + dot16(high, parts_ref[2])
        moved = complex_rows(top[:size] + (top[size : 2 * size] + mid[:size] + small), count, rows)
        factor = inverse_factor(*hermitian_parts(dot_nt(block, block), count), count)
        factor_ref[...] = factor
        vectors[later, me] = dot_nn(factor, moved)
        send_staged(vectors.at[later], vec_send.at[later], vec_recv.at[later])
        return carry

    lax.fori_loop(0, SUB_ITERS, subspace_round, 0)
    last, after = (SUB_ITERS - 1) % 2, SUB_ITERS % 2
    flag = flag_ref[...].astype(jnp.float32)
    basis = dot_nn(factor_ref[...], whole(vectors.at[last])) * flag
    basis_ref[...] = basis
    arrive_staged(vectors.at[after], vec_send.at[after], vec_recv.at[after])
    image = whole(vectors.at[after]) * flag
    inner = embed(*hermitian_parts(dot_nt(image, basis), count))
    wide_ref[0 : 2 * count, :] = image - 0.5 * dot_nn(inner, basis)
    wide_ref[2 * count :, :] = basis
    own_basis = basis_ref[:, own]
    own_wide = wide_ref[0 : 2 * count, own]
    left_real = jnp.concatenate([own_basis, own_wide], 0)
    left_imag = jnp.concatenate(
        [own_basis[count:], -own_basis[:count], own_wide[count:], -own_wide[:count]], 0
    )
    left = jnp.concatenate([left_real.T, left_imag.T], 0)

    @pl.loop(0, peers)
    def _(j):
        part = pl.ds(pl.multiple_of(j * rows, rows), rows)
        projected = cov_ref[:, part] - dot_nn(left, wide_ref[:, part])
        high, low = split_halves(projected.T)
        parts_ref[0, part, :] = high
        parts_ref[1, part, :] = low

    arrive(traces, tr_send, tr_recv)
    trace = traces[0, 0:1, 0:1]
    for j in range(1, peers):
        trace = trace + traces[j, 0:1, 0:1]
    load = diagonal_loading * trace / antennas

    def inner_product(a, b):
        each = jnp.sum(a * b, axis=1, keepdims=True)
        return each[:beams] + each[beams:]

    def both(each):
        return jnp.concatenate([each, each], 0)

    steering = steer_ref[...]
    x_ref[...] = jnp.zeros_like(steering)
    r_ref[...] = steering
    p_ref[...] = steering

    def cg_step(step, norm):
        slot = lax.rem(step, 2)
        direction = p_ref[...]
        high, low = split_halves(direction)
        top = dot16(jnp.concatenate([high, low], 0), parts_ref[0])
        product = top[: 2 * beams] + top[2 * beams :] + dot16(high, parts_ref[1])
        mapped[slot, me] = complex_rows(product, beams, rows)
        send(mapped.at[slot], map_send.at[slot], map_recv.at[slot])
        arrive(mapped.at[slot], map_send.at[slot], map_recv.at[slot])
        combined = whole(mapped.at[slot]) + load * direction
        alpha = norm / inner_product(direction, combined)
        alpha_rows = both(alpha)
        x_ref[...] = x_ref[...] + alpha_rows * direction
        residual = r_ref[...] - alpha_rows * combined
        r_ref[...] = residual
        new_norm = inner_product(residual, residual)
        p_ref[...] = residual + both(new_norm / norm) * direction
        return new_norm

    lax.fori_loop(0, CG_ITERS, cg_step, inner_product(steering, steering))
    response = both(inner_product(steer_ref[...], x_ref[...]))
    out_ref[...] = antennas * x_ref[:, own] / response


def beam_weights(covariance, rfi_flags, beam_steer_index, start_columns):
    peers = lax.axis_size("tile")
    _, _, rows, antennas = covariance.shape
    beams = beam_steer_index.shape[1]
    count = start_columns.shape[1]
    steering = steering_table(beam_steer_index[0], antennas).reshape(2 * beams, antennas)
    f32, b16 = jnp.float32, jnp.bfloat16
    dma = pltpu.SemaphoreType.DMA
    out = pl.pallas_call(
        functools.partial(tail_kernel, peers),
        out_shape=jax.ShapeDtypeStruct((2 * beams, rows), f32),
        in_specs=[pl.BlockSpec(memory_space=pltpu.VMEM)] * 4,
        out_specs=pl.BlockSpec(memory_space=pltpu.VMEM),
        scratch_shapes=[
            pltpu.VMEM((2, peers, 2 * count, rows), f32),
            pltpu.VMEM((2, peers, 2 * beams, rows), f32),
            pltpu.VMEM((peers, 8, 128), f32),
            pltpu.VMEM((2 * count, 2 * count), f32),
            pltpu.VMEM((2 * count, antennas), f32),
            pltpu.VMEM((4 * count, antennas), f32),
            pltpu.VMEM((3, antennas, 2 * rows), b16),
            pltpu.VMEM((2 * beams, antennas), f32),
            pltpu.VMEM((2 * beams, antennas), f32),
            pltpu.VMEM((2 * beams, antennas), f32),
            dma((2, peers)),
            dma((2, peers)),
            dma((2, peers)),
            dma((2, peers)),
            dma((peers,)),
            dma((peers,)),
        ],
        compiler_params=pltpu.CompilerParams(
            collective_id=0, has_side_effects=True, vmem_limit_bytes=48 * 1024 * 1024
        ),
    )(
        covariance.reshape(2 * rows, antennas),
        start_columns.reshape(count, 1),
        rfi_flags.reshape(1, 1),
        steering,
    )
    return jnp.swapaxes(out.reshape(2, beams, rows), 0, 1)[None]


def shards(voltages, rfi_flags, beam_steer_index, start_columns):
    covariance = channel_covariance(voltages)
    weights = beam_weights(covariance, rfi_flags, beam_steer_index, start_columns)
    return (covariance, weights)


def solution(mesh):
    in_specs = (P(None, None, "tile", "chan"), P("chan"), P("chan", None), P("chan", None))
    out_specs = (P("chan", None, "tile", None), P("chan", None, None, "tile"))
    return jax.shard_map(shards, mesh=mesh, in_specs=in_specs, out_specs=out_specs, check_vma=False)
```

```python
import functools
import math

import jax
import jax.numpy as jnp
from jax import lax
from jax.experimental import pallas as pl
from jax.experimental.pallas import tpu as pltpu
from jax.sharding import PartitionSpec as P

SUB_ITERS = 4
CG_ITERS = 12


diagonal_loading = 0.1
highest = lax.Precision.HIGHEST
MESH = pl.DeviceIdType.MESH


def steering_table(beam_entries, element_total):
    element_index = jnp.arange(element_total, dtype=jnp.int32)
    steer_phases = (beam_entries[..., None] * element_index % element_total).astype(
        jnp.float32
    ) * (2.0 * math.pi / element_total)
    return jnp.stack([jnp.cos(steer_phases), jnp.sin(steer_phases)], axis=0)


def dot_nt(a, b):
    return lax.dot_general(
        a, b, (((1,), (1,)), ((), ())), precision=highest, preferred_element_type=jnp.float32
    )


def dot_nn(a, b):
    return lax.dot_general(
        a, b, (((1,), (0,)), ((), ())), precision=highest, preferred_element_type=jnp.float32
    )


def dot16(a, b):
    return jnp.dot(a, b, preferred_element_type=jnp.float32)


def split_thirds(values):
    high = values.astype(jnp.bfloat16)
    rest = values - high.astype(jnp.float32)
    middle = rest.astype(jnp.bfloat16)
    low = (rest - middle.astype(jnp.float32)).astype(jnp.bfloat16)
    return high, middle, low


def split_halves(values):
    high = values.astype(jnp.bfloat16)
    low = (values - high.astype(jnp.float32)).astype(jnp.bfloat16)
    return high, low


def complex_rows(product, count, rows):
    real = product[:count, :rows] - product[count:, rows:]
    imag = product[count:, :rows] + product[:count, rows:]
    return jnp.concatenate([real, imag], 0)


def embed(real, imag):
    return jnp.concatenate(
        [jnp.concatenate([real, -imag], 1), jnp.concatenate([imag, real], 1)], 0
    )


def hermitian_parts(product, count):
    real = product[:count, :count] + product[count:, count:]
    imag = product[count:, :count] - product[:count, count:]
    return real, imag


def inverse_factor(gram_real, gram_imag, count):
    row_id = lax.broadcasted_iota(jnp.int32, (count, count), 0)
    col_id = lax.broadcasted_iota(jnp.int32, (count, count), 1)
    eye = (row_id == col_id).astype(jnp.float32)
    system = jnp.concatenate([gram_real, gram_imag, eye, jnp.zeros_like(eye)], 1)
    below = lax.broadcasted_iota(jnp.int32, (count, 1), 0)
    lane = lax.broadcasted_iota(jnp.int32, (1, 4 * count), 1)
    first_half = lax.rem(lane, 2 * count) < count
    for k in range(count):
        row = system[k : k + 1, :]
        fore = pltpu.roll(row, 3 * count, 1)
        back = pltpu.roll(row, count, 1)
        turned = jnp.where(first_half, -fore, back)
        scale = jnp.where(below > k, 1.0 / row[:, k : k + 1], 0.0)
        factor_real = system[:, k : k + 1] * scale
        factor_imag = system[:, count + k : count + k + 1] * scale
        system = system - factor_real * row - factor_imag * turned
    pivots = jnp.sum(system[:, :count] * eye, axis=1, keepdims=True)
    system = system * lax.rsqrt(pivots)
    return embed(system[:, 2 * count : 3 * count], system[:, 3 * count :])


def ring_place(position, peers):
    half = peers // 2
    return jnp.where(position < half, 2 * position, 2 * (peers - 1 - position) + 1)


def covariance_kernel(
    peers, groups, volt_ref, cov_ref, shards_ref, left_ref, local_sem, turn_send, turn_recv, ring_send, ring_recv
):
    me = lax.axis_index("tile")
    chan = lax.axis_index("chan")
    _, _, depth, width = volt_ref.shape
    rows = cov_ref.shape[0] // 2
    antennas = cov_ref.shape[1]
    half = peers // 2
    own = pl.ds(pl.multiple_of(me * rows, rows), rows)
    odd = lax.rem(me, 2)
    position = jnp.where(odd == 0, me // 2, peers - 1 - me // 2)

    def tile_at(offset):
        return ring_place(lax.rem(position + offset + peers, peers), peers)

    right, left = tile_at(1), tile_at(-1)

    barrier = pltpu.get_barrier_semaphore()
    for k in range(1, groups):
        pl.semaphore_signal(
            barrier, inc=1, device_id={"chan": lax.rem(chan + k, groups)}, device_id_type=MESH
        )
    for neighbour in (left, right):
        pl.semaphore_signal(barrier, inc=1, device_id={"tile": neighbour}, device_id_type=MESH)
    pl.semaphore_wait(barrier, groups + 1)

    def piece(tile, source):
        lanes = pl.ds(pl.multiple_of(source * width, width), width)
        return shards_ref.at[tile, :, :, lanes]

    def turn_copy(k):
        return pltpu.make_async_remote_copy(
            src_ref=volt_ref.at[lax.rem(chan + k, groups)],
            dst_ref=piece(me, chan),
            send_sem=turn_send.at[k],
            recv_sem=turn_recv.at[k],
            device_id={"chan": lax.rem(chan + k, groups)},
            device_id_type=MESH,
        )

    def turn_arrival(k):
        source = lax.rem(chan - k + groups, groups)
        return pltpu.make_async_remote_copy(
            src_ref=volt_ref.at[chan],
            dst_ref=piece(me, source),
            send_sem=turn_send.at[k],
            recv_sem=turn_recv.at[k],
            device_id={"chan": lax.rem(chan + k, groups)},
            device_id_type=MESH,
        )

    def hops(way, k):
        longer = 0 if k < groups // 2 else 1
        return half if way == longer else half - 1

    def ring_copy(way, hop, k, arriving=False):
        step = 1 if way == 0 else -1
        tile = tile_at(-step * (hop + 1 if arriving else hop))
        part = piece(tile, lax.rem(chan - k + groups, groups))
        return pltpu.make_async_remote_copy(
            src_ref=part,
            dst_ref=part,
            send_sem=ring_send.at[way, hop, k],
            recv_sem=ring_recv.at[way, hop, k],
            device_id={"tile": right if way == 0 else left},
            device_id_type=MESH,
        )

    def add_shard(tile, first=False, scale=None):
        real, imag = shards_ref[tile, 0, :, own], shards_ref[tile, 1, :, own]
        left_ref[...] = jnp.concatenate(
            [jnp.concatenate([real, imag], 1), jnp.concatenate([imag, -real], 1)], 0
        ).T

        @pl.loop(0, peers)
        def _(j):
            part = pl.ds(pl.multiple_of(j * rows, rows), rows)
            right_part = jnp.concatenate(
                [shards_ref[tile, 0, :, part], shards_ref[tile, 1, :, part]], 0
            )
            term = jnp.dot(left_ref[...], right_part, preferred_element_type=jnp.float32)
            if not first:
                term = term + cov_ref[:, part]
            if scale is not None:
                term = term * scale
            cov_ref[:, part] = term

    local = pltpu.make_async_copy(volt_ref.at[chan], piece(me, chan), local_sem)
    for k in range(1, groups):
        turn_copy(k).start()
    local.start()
    for k in range(groups):
        if k == 0:
            local.wait()
        else:
            turn_arrival(k).wait_recv()
        for way in range(2):
            ring_copy(way, 0, k).start()
    add_shard(me, first=True)
    for hop in range(half):
        for k in range(groups):
            for way in range(2):
                if hop < hops(way, k):
                    ring_copy(way, hop, k, arriving=True).wait_recv()
                    if hop + 1 < hops(way, k):
                        ring_copy(way, hop + 1, k).start()
        if hop + 1 < half:
            add_shard(tile_at(-hop - 1))
            add_shard(tile_at(hop + 1))
        else:
            add_shard(tile_at(half), scale=1.0 / (depth * peers))
    for k in range(1, groups):
        turn_copy(k).wait_send()
    for k in range(groups):
        for way in range(2):
            for hop in range(hops(way, k)):
                ring_copy(way, hop, k).wait_send()


def channel_covariance(voltages):
    peers, groups = lax.axis_size("tile"), lax.axis_size("chan")
    _, _, depth, width = voltages.shape
    antennas = width * groups
    rows = antennas // peers
    dma = pltpu.SemaphoreType.DMA
    out = pl.pallas_call(
        functools.partial(covariance_kernel, peers, groups),
        out_shape=jax.ShapeDtypeStruct((2 * rows, antennas), jnp.float32),
        in_specs=[pl.BlockSpec(memory_space=pl.ANY)],
        out_specs=pl.BlockSpec(memory_space=pltpu.VMEM),
        scratch_shapes=[
            pltpu.VMEM((peers, 2, depth, antennas), voltages.dtype),
            pltpu.VMEM((2 * rows, 2 * depth), voltages.dtype),
            dma(()),
            dma((groups,)),
            dma((groups,)),
            dma((2, peers // 2, groups)),
            dma((2, peers // 2, groups)),
        ],
        compiler_params=pltpu.CompilerParams(
            collective_id=1, has_side_effects=True, vmem_limit_bytes=40 * 1024 * 1024
        ),
    )(voltages)
    return out.reshape(1, 2, rows, antennas)


def tail_kernel(
    peers,
    cov_ref,
    columns_ref,
    flag_ref,
    steer_ref,
    out_ref,
    vectors,
    mapped,
    traces,
    factor_ref,
    basis_ref,
    wide_ref,
    parts_ref,
    x_ref,
    r_ref,
    p_ref,
    vec_send,
    vec_recv,
    map_send,
    map_recv,
    tr_send,
    tr_recv,
):
    me = lax.axis_index("tile")
    rows = cov_ref.shape[0] // 2
    antennas = cov_ref.shape[1]
    count = columns_ref.shape[0]
    beams = steer_ref.shape[0] // 2
    own = pl.ds(pl.multiple_of(me * rows, rows), rows)

    barrier = pltpu.get_barrier_semaphore()
    for k in range(1, peers):
        pl.semaphore_signal(
            barrier, inc=1, device_id={"tile": lax.rem(me + k, peers)}, device_id_type=MESH
        )
    pl.semaphore_wait(barrier, peers - 1)

    def send(block, send_sem, recv_sem):
        for k in range(1, peers):
            pltpu.make_async_remote_copy(
                src_ref=block.at[me],
                dst_ref=block.at[me],
                send_sem=send_sem.at[k],
                recv_sem=recv_sem.at[k],
                device_id={"tile": lax.rem(me + k, peers)},
                device_id_type=MESH,
            ).start()

    def arrive(block, send_sem, recv_sem):
        for k in range(1, peers):
            source = lax.rem(me - k + peers, peers)
            copy = pltpu.make_async_remote_copy(
                src_ref=block.at[me],
                dst_ref=block.at[source],
                send_sem=send_sem.at[k],
                recv_sem=recv_sem.at[k],
                device_id={"tile": lax.rem(me + k, peers)},
                device_id_type=MESH,
            )
            copy.wait_send()
            copy.wait_recv()

    half = peers // 2
    line, side = me // 2, lax.rem(me, 2)
    partner = 2 * line + 1 - side

    def hand_over(block, tile, landed, target, send_sem, recv_sem, index):
        return pltpu.make_async_remote_copy(
            src_ref=block.at[tile],
            dst_ref=block.at[landed],
            send_sem=send_sem.at[index],
            recv_sem=recv_sem.at[index],
            device_id={"tile": target},
            device_id_type=MESH,
        )

    def along(k):
        return 2 * lax.rem(line + k + half, half) + side

    def send_staged(block, send_sem, recv_sem):
        for k in range(1, half):
            hand_over(block, me, me, along(k), send_sem, recv_sem, k).start()
        hand_over(block, me, me, partner, send_sem, recv_sem, half).start()

    def arrive_staged(block, send_sem, recv_sem):
        for k in range(1, half):
            source = along(-k)
            hand_over(block, me, source, along(k), send_sem, recv_sem, k).wait_recv()
            hand_over(block, source, source, partner, send_sem, recv_sem, half + k).start()
        for k in range(half):
            source = along(-k)
            across = 2 * (source // 2) + 1 - side
            hand_over(block, source, across, partner, send_sem, recv_sem, half + k).wait_recv()
            hand_over(block, source, source, partner, send_sem, recv_sem, half + k).wait_send()
        for k in range(1, half):
            hand_over(block, me, me, along(k), send_sem, recv_sem, k).wait_send()

    def whole(block):
        return jnp.concatenate([block[j] for j in range(peers)], 1)

    @pl.loop(0, peers)
    def _(j):
        part = pl.ds(pl.multiple_of(j * rows, rows), rows)
        thirds = split_thirds(cov_ref[:, part].T)
        for third, values in enumerate(thirds):
            parts_ref[third, part, :] = values

    hot = jnp.where(
        lax.broadcasted_iota(jnp.int32, (count, antennas), 1) == columns_ref[...], 1.0, 0.0
    ).astype(jnp.bfloat16)
    picked = dot16(hot, parts_ref[0]) + (dot16(hot, parts_ref[1]) + dot16(hot, parts_ref[2]))
    vectors[0, me] = jnp.concatenate([picked[:, :rows], picked[:, rows:]], 0)
    send_staged(vectors.at[0], vec_send.at[0], vec_recv.at[0])

    square = cov_ref[0:rows, own]
    on_diagonal = lax.broadcasted_iota(jnp.int32, (rows, rows), 0) == lax.broadcasted_iota(
        jnp.int32, (rows, rows), 1
    )
    own_trace = jnp.sum(jnp.where(on_diagonal, square, 0.0), axis=(0, 1), keepdims=True)
    traces[me] = jnp.broadcast_to(own_trace, traces.shape[1:])
    send(traces, tr_send, tr_recv)

    def subspace_round(step, carry):
        now, later = lax.rem(step, 2), lax.rem(step + 1, 2)
        arrive_staged(vectors.at[now], vec_send.at[now], vec_recv.at[now])
        block = whole(vectors.at[now])
        size = 2 * count
        high, middle, low = split_thirds(block)
        top = dot16(jnp.concatenate([high, middle, low], 0), parts_ref[0])
        mid = dot16(jnp.concatenate([high, middle], 0), parts_ref[1])
        small = top[2 * size :] + mid[size:] + dot16(high, parts_ref[2])
        moved = complex_rows(top[:size] + (top[size : 2 * size] + mid[:size] + small), count, rows)
        factor = inverse_factor(*hermitian_parts(dot_nt(block, block), count), count)
        factor_ref[...] = factor
        vectors[later, me] = dot_nn(factor, moved)
        send_staged(vectors.at[later], vec_send.at[later], vec_recv.at[later])
        return carry

    lax.fori_loop(0, SUB_ITERS, subspace_round, 0)
    last, after = (SUB_ITERS - 1) % 2, SUB_ITERS % 2
    flag = flag_ref[...].astype(jnp.float32)
    basis = dot_nn(factor_ref[...], whole(vectors.at[last])) * flag
    basis_ref[...] = basis
    arrive_staged(vectors.at[after], vec_send.at[after], vec_recv.at[after])
    image = whole(vectors.at[after]) * flag
    inner = embed(*hermitian_parts(dot_nt(image, basis), count))
    wide_ref[0 : 2 * count, :] = image - 0.5 * dot_nn(inner, basis)
    wide_ref[2 * count :, :] = basis
    own_basis = basis_ref[:, own]
    own_wide = wide_ref[0 : 2 * count, own]
    left_real = jnp.concatenate([own_basis, own_wide], 0)
    left_imag = jnp.concatenate(
        [own_basis[count:], -own_basis[:count], own_wide[count:], -own_wide[:count]], 0
    )
    left = jnp.concatenate([left_real.T, left_imag.T], 0)

    @pl.loop(0, peers)
    def _(j):
        part = pl.ds(pl.multiple_of(j * rows, rows), rows)
        projected = cov_ref[:, part] - dot_nn(left, wide_ref[:, part])
        high, low = split_halves(projected.T)
        parts_ref[0, part, :] = high
        parts_ref[1, part, :] = low

    arrive(traces, tr_send, tr_recv)
    trace = traces[0, 0:1, 0:1]
    for j in range(1, peers):
        trace = trace + traces[j, 0:1, 0:1]
    load = diagonal_loading * trace / antennas

    def inner_product(a, b):
        each = jnp.sum(a * b, axis=1, keepdims=True)
        return each[:beams] + each[beams:]

    def both(each):
        return jnp.concatenate([each, each], 0)

    steering = steer_ref[...]
    x_ref[...] = jnp.zeros_like(steering)
    r_ref[...] = steering
    p_ref[...] = steering

    def cg_step(step, norm):
        slot = lax.rem(step, 2)
        direction = p_ref[...]
        high, low = split_halves(direction)
        top = dot16(jnp.concatenate([high, low], 0), parts_ref[0])
        product = top[: 2 * beams] + top[2 * beams :] + dot16(high, parts_ref[1])
        mapped[slot, me] = complex_rows(product, beams, rows)
        send_staged(mapped.at[slot], map_send.at[slot], map_recv.at[slot])
        arrive_staged(mapped.at[slot], map_send.at[slot], map_recv.at[slot])
        combined = whole(mapped.at[slot]) + load * direction
        alpha = norm / inner_product(direction, combined)
        alpha_rows = both(alpha)
        x_ref[...] = x_ref[...] + alpha_rows * direction
        residual = r_ref[...] - alpha_rows * combined
        r_ref[...] = residual
        new_norm = inner_product(residual, residual)
        p_ref[...] = residual + both(new_norm / norm) * direction
        return new_norm

    lax.fori_loop(0, CG_ITERS, cg_step, inner_product(steering, steering))
    response = both(inner_product(steer_ref[...], x_ref[...]))
    out_ref[...] = antennas * x_ref[:, own] / response


def beam_weights(covariance, rfi_flags, beam_steer_index, start_columns):
    peers = lax.axis_size("tile")
    _, _, rows, antennas = covariance.shape
    beams = beam_steer_index.shape[1]
    count = start_columns.shape[1]
    steering = steering_table(beam_steer_index[0], antennas).reshape(2 * beams, antennas)
    f32, b16 = jnp.float32, jnp.bfloat16
    dma = pltpu.SemaphoreType.DMA
    out = pl.pallas_call(
        functools.partial(tail_kernel, peers),
        out_shape=jax.ShapeDtypeStruct((2 * beams, rows), f32),
        in_specs=[pl.BlockSpec(memory_space=pltpu.VMEM)] * 4,
        out_specs=pl.BlockSpec(memory_space=pltpu.VMEM),
        scratch_shapes=[
            pltpu.VMEM((2, peers, 2 * count, rows), f32),
            pltpu.VMEM((2, peers, 2 * beams, rows), f32),
            pltpu.VMEM((peers, 8, 128), f32),
            pltpu.VMEM((2 * count, 2 * count), f32),
            pltpu.VMEM((2 * count, antennas), f32),
            pltpu.VMEM((4 * count, antennas), f32),
            pltpu.VMEM((3, antennas, 2 * rows), b16),
            pltpu.VMEM((2 * beams, antennas), f32),
            pltpu.VMEM((2 * beams, antennas), f32),
            pltpu.VMEM((2 * beams, antennas), f32),
            dma((2, peers)),
            dma((2, peers)),
            dma((2, peers)),
            dma((2, peers)),
            dma((peers,)),
            dma((peers,)),
        ],
        compiler_params=pltpu.CompilerParams(
            collective_id=0, has_side_effects=True, vmem_limit_bytes=48 * 1024 * 1024
        ),
    )(
        covariance.reshape(2 * rows, antennas),
        start_columns.reshape(count, 1),
        rfi_flags.reshape(1, 1),
        steering,
    )
    return jnp.swapaxes(out.reshape(2, beams, rows), 0, 1)[None]


def shards(voltages, rfi_flags, beam_steer_index, start_columns):
    covariance = channel_covariance(voltages)
    weights = beam_weights(covariance, rfi_flags, beam_steer_index, start_columns)
    return (covariance, weights)


def solution(mesh):
    in_specs = (P(None, None, "tile", "chan"), P("chan"), P("chan", None), P("chan", None))
    out_specs = (P("chan", None, "tile", None), P("chan", None, None, "tile"))
    return jax.shard_map(shards, mesh=mesh, in_specs=in_specs, out_specs=out_specs, check_vma=False)
```
